32 devices in a mesh: dp: 8 (over y, x, core), tok: 4 (over z).
Axes of the slice: x: 2, y: 2, z: 4, core: 2. Of those that a mesh axis runs over, the one named last changes fastest.
Arguments:
- student_hidden: bfloat16 [16, 1024, 2048], P('dp', 'tok'), may hold values from -48 to 48
- teacher_values: bfloat16 [16, 1024, 4096], P('dp', 'tok'), may hold values from -48 to 48
- value_weight: bfloat16 [2048, 2048], P(None, 'tok'), may hold values from -0.09375 to 0.09375
- value_bias: bfloat16 [1, 2048], P(None, 'tok'), may hold values from -3 to 3
Outputs:
- hidden_grad: bfloat16 [16, 1024, 2048], P('dp', 'tok')
- bias_grad: float32 [2048], P('tok')
The draws below stay inside these ranges and needn't reach their ends.
All inputs are finite; a program needn't handle non-finite values.
Results may differ from the reference program's by a relative error of at most 0.012.
The reference program's roundings to bfloat16 on the way (of `student_values`, `score_grad` and `value_grad`) count: a program that leaves them out, or rounds other values in their place, can miss the bound.
Values may be sent and summed in bfloat16 or wider, within the bound.
A program may use at most 64 MiB of HBM per device.

```python
import jax
import jax.numpy as jnp
from jax import lax

DS = 2048
HEADS = 32
SH = 64
TH = 128
LENGTH = 1024
DV = 2048
TW = 4096
SEQS = 16


def shaped_rows(key, width, base_scale):
    first = jax.random.fold_in(key, 0)
    base = jax.random.normal(first, (SEQS, LENGTH, width), jnp.float32)
    return jnp.clip(base_scale * base, -48.0, 48.0)


def draw_student_hidden(key, part):
    return shaped_rows(jax.random.fold_in(key, 11), DS, 1.0).astype(jnp.bfloat16)


def draw_teacher_values(key, part):
    return shaped_rows(jax.random.fold_in(key, 23), TW, 0.7).astype(jnp.bfloat16)


def block_scale(stream_key, extent, cuts, low, high):
    def one(axis_at, blocks):
        heights = jax.random.uniform(jax.random.fold_in(jax.random.fold_in(stream_key, 6), axis_at), (blocks,), jnp.float32, low / len(cuts), high / len(cuts))
        return jnp.repeat(jnp.exp(heights), extent[axis_at] // blocks).reshape((-1,) + (1,) * (len(extent) - axis_at - 1))

    loudness = one(*cuts[0])
    for cut in cuts[1:]:
        loudness = loudness * one(*cut)
    return loudness


def bell_draw(key, dims, deviation, bound, cuts=(), held_as=jnp.bfloat16):
    values = deviation * jax.random.normal(key, dims, jnp.float32)
    if cuts:
        values = values * block_scale(key, dims, cuts, -0.22, 0.18)
    return jnp.clip(values, -bound, bound).astype(held_as)


def setup_inputs(seed: int = 0) -> dict:
    splits = jax.random.split(jax.random.key(seed), 5)
    return {
        "student_hidden": draw_student_hidden(jax.random.fold_in(splits[4], 71), 0),
        "teacher_values": draw_teacher_values(jax.random.fold_in(splits[4], 71), 0),
        "value_weight": bell_draw(splits[2], (DS, DV), (2 * DS) ** -0.5, 0.09375, ((1, 4),)),
        "value_bias": bell_draw(splits[3], (1, DV), 0.5, 3.0, ((1, 4),)),
    }


def head_grads(student_head, teacher_head):
    teacher_scores = jnp.dot(teacher_head, teacher_head.T, preferred_element_type=jnp.float32) / jnp.sqrt(jnp.float32(TH))
    teacher_prob = jax.nn.softmax(teacher_scores, axis=-1)
    student_scores = jnp.dot(student_head, student_head.T, preferred_element_type=jnp.float32) / jnp.sqrt(jnp.float32(SH))
    student_prob = jax.nn.softmax(student_scores, axis=-1)
    score_grad = (LENGTH * (student_prob - teacher_prob)).astype(jnp.bfloat16)
    summed = jnp.dot(score_grad, student_head, preferred_element_type=jnp.float32) + jnp.dot(score_grad.T, student_head, preferred_element_type=jnp.float32)
    return (summed / jnp.sqrt(jnp.float32(SH))).astype(jnp.bfloat16)

def reference(student_hidden, teacher_values, value_weight, value_bias):
    rows = student_hidden.reshape(SEQS * LENGTH, DS)
    student_values = (jnp.dot(rows, value_weight, preferred_element_type=jnp.float32) + value_bias.astype(jnp.float32)).astype(jnp.bfloat16)
    student_items = student_values.reshape(SEQS, LENGTH, HEADS, SH).transpose(0, 2, 1, 3).reshape(SEQS * HEADS, LENGTH, SH)
    teacher_items = teacher_values.reshape(SEQS, LENGTH, HEADS, TH).transpose(0, 2, 1, 3).reshape(SEQS * HEADS, LENGTH, TH)
    grads = lax.map(lambda pair: head_grads(pair[0], pair[1]), (student_items, teacher_items))
    value_grad = grads.reshape(SEQS, HEADS, LENGTH, SH).transpose(0, 2, 1, 3).reshape(SEQS * LENGTH, DV)
    hidden_grad = jnp.dot(value_grad, value_weight.T, preferred_element_type=jnp.float32).astype(jnp.bfloat16)
    bias_grad = lax.optimization_barrier(jnp.sum(value_grad.astype(jnp.float32), axis=0)) / jnp.sqrt(jnp.float32(SEQS * LENGTH))
    return (hidden_grad.reshape(SEQS, LENGTH, DS), bias_grad)
```

```python
import functools
import math

import jax
import jax.numpy as jnp
from jax import lax
from jax.experimental import pallas as pl
from jax.experimental.pallas import tpu as pltpu
from jax.sharding import PartitionSpec as P

SH = 64
TH = 128
PAIR = 128
HEADS_PER = PAIR // SH
LOG2E = math.log2(math.e)


def aligned(index, step):
    return pl.ds(pl.multiple_of(index * step, step), step)


def kernel(
    n_tok, n_dp, seqs, local,
    hidden, teacher, weight, bias,
    out, bias_out,
    w_full, t_full, s_send, s_full, g_buf, vg, bias_all, bsum,
    t_tr, s_tr, s_mask, acc, acc_tr,
    wsend, wrecv, dsend, drecv, csend, crecv, bsend, brecv,
    tsend, trecv, ssend, srecv, gsend, grecv, rsend, rrecv, lsem,
):
    tok = lax.axis_index("tok")
    dp = lax.axis_index("dp")
    width = hidden.shape[1]
    cols = weight.shape[1]
    tcols = teacher.shape[2] // n_tok
    length = n_tok * local
    slice_rows = width // n_dp
    pairs = cols // PAIR
    half = n_dp // 2
    core = lax.rem(dp, 2)
    sibling = dp + 1 - 2 * core

    def tok_at(k):
        return lax.rem(tok + k, n_tok)

    def same_core(k):
        return lax.rem(dp + 2 * k, n_dp)

    def remote(src, dst, send, recv, **where):
        return pltpu.make_async_remote_copy(
            src_ref=src, dst_ref=dst, send_sem=send, recv_sem=recv,
            device_id=where, device_id_type=pl.DeviceIdType.MESH,
        )

    def w_copy(k):
        return remote(
            weight.at[aligned(dp, slice_rows), :],
            w_full.at[aligned(dp, slice_rows), aligned(tok, cols)],
            wsend.at[k], wrecv.at[k], tok=tok_at(k),
        )

    def d_copy(k):
        block = w_full.at[aligned(dp, slice_rows), :]
        return remote(block, block, dsend.at[k], drecv.at[k], dp=same_core(k))

    def c_copy(k):
        owner = lax.rem(dp - 2 * k + n_dp, n_dp)
        block = w_full.at[aligned(owner, slice_rows), :]
        return remote(block, block, csend.at[k], crecv.at[k], dp=sibling)

    def b_copy(k):
        return remote(bias_all.at[tok], bias_all.at[tok], bsend.at[k], brecv.at[k], tok=tok_at(k))

    def t_copy(s, k):
        return remote(
            teacher.at[s, :, aligned(tok_at(k), tcols)],
            t_full.at[s, aligned(tok, local), :],
            tsend.at[s, k], trecv.at[s, k], tok=tok_at(k),
        )

    def s_copy(s, k):
        return remote(
            s_send.at[k, s], s_full.at[s, aligned(tok, local), :],
            ssend.at[s, k], srecv.at[s, k], tok=tok_at(k),
        )

    def g_copy(s, j, k):
        return remote(
            g_buf.at[s, aligned(tok_at(k), local), aligned(j, PAIR)],
            vg.at[s, :, aligned(tok * pairs + j, PAIR)],
            gsend.at[s, j, k], grecv.at[s, j, k], tok=tok_at(k),
        )

    def r_copy(k):
        return remote(bsum.at[dp], bsum.at[dp], rsend.at[k], rrecv.at[k], dp=lax.rem(dp + k, n_dp))

    def own_w():
        return pltpu.make_async_copy(
            weight.at[aligned(dp, slice_rows), :],
            w_full.at[aligned(dp, slice_rows), aligned(tok, cols)], lsem.at[0],
        )

    def own_t(s):
        return pltpu.make_async_copy(
            teacher.at[s, :, aligned(tok, tcols)], t_full.at[s, aligned(tok, local), :], lsem.at[1 + s]
        )

    barrier = pltpu.get_barrier_semaphore()
    for k in range(1, n_tok):
        pl.semaphore_signal(barrier, inc=1, device_id={"tok": tok_at(k)}, device_id_type=pl.DeviceIdType.MESH)
    for k in range(1, n_dp):
        pl.semaphore_signal(
            barrier, inc=1, device_id={"dp": lax.rem(dp + k, n_dp)}, device_id_type=pl.DeviceIdType.MESH
        )
    bias_all[tok] = bias[...]
    own_w().start()
    for s in range(seqs):
        own_t(s).start()
    pl.semaphore_wait(barrier, n_tok + n_dp - 2)

    for k in range(1, n_tok):
        w_copy(k).start()
        b_copy(k).start()
    own_w().wait()
    for k in range(1, n_tok):
        w_copy(k).wait_recv()
    for k in range(1, half):
        d_copy(k).start()
    c_copy(0).start()
    for s in range(seqs):
        for k in range(1, n_tok):
            t_copy(s, k).start()
    for k in range(1, half):
        d_copy(k).wait_recv()
        c_copy(k).start()
    for k in range(half):
        c_copy(k).wait_recv()
    for k in range(1, n_tok):
        b_copy(k).wait_recv()

    def project(step, carry):
        k = lax.rem(step + 1, n_tok)
        p = tok_at(k)
        values = jnp.dot(hidden[...], w_full[:, aligned(p, cols)], preferred_element_type=jnp.float32)
        values = (values + bias_all[p][0:1, :]).astype(jnp.bfloat16)

        @pl.when(k > 0)
        def _():
            for s in range(seqs):
                s_send[k, s] = values[s * local : (s + 1) * local]
                s_copy(s, k).start()

        @pl.when(k == 0)
        def _():
            for s in range(seqs):
                s_full[s, aligned(tok, local), :] = values[s * local : (s + 1) * local]

        return carry

    lax.fori_loop(0, n_tok, project, 0)

    block = min(256, length)
    lane_head = lax.broadcasted_iota(jnp.int32, (length, PAIR), 1) // SH
    t_scale = LOG2E / math.sqrt(TH)
    s_scale = LOG2E / math.sqrt(SH)

    def softmax_terms(scores, scale):
        top = jnp.max(scores, axis=1, keepdims=True)
        terms = jnp.exp2((scores - top) * scale)
        return terms, length / jnp.sum(terms, axis=1, keepdims=True)

    def unit(s, j):
        values = s_full[s, :, aligned(j, PAIR)]
        s_tr[...] = values.T
        for h in range(HEADS_PER):
            s_mask[h] = jnp.where(lane_head == h, values, jnp.zeros_like(values))
            t_tr[h] = t_full[s, :, aligned(j * HEADS_PER + h, TH)].T
        acc_tr[...] = jnp.zeros_like(acc_tr)

        def query(i, carry):
            rows = aligned(i, block)
            total = None
            for h in range(HEADS_PER):
                t_scores = jnp.dot(
                    t_full[s, rows, aligned(j * HEADS_PER + h, TH)], t_tr[h], preferred_element_type=jnp.float32
                )
                s_scores = jnp.dot(s_mask[h, rows, :], s_tr[...], preferred_element_type=jnp.float32)
                t_terms, t_norm = softmax_terms(t_scores, t_scale)
                s_terms, s_norm = softmax_terms(s_scores, s_scale)
                grad = (s_terms * s_norm - t_terms * t_norm).astype(jnp.bfloat16)
                part = jnp.dot(grad, s_mask[h], preferred_element_type=jnp.float32)
                total = part if total is None else total + part
                acc_tr[h * SH : (h + 1) * SH, :] += jnp.dot(
                    s_tr[h * SH : (h + 1) * SH, rows], grad, preferred_element_type=jnp.float32
                )
            acc[rows, :] = total
            return carry

        lax.fori_loop(0, length // block, query, 0)
        result = ((acc[...] + acc_tr[...].T) * (1.0 / math.sqrt(SH))).astype(jnp.bfloat16)
        g_buf[s, :, aligned(j, PAIR)] = result
        part = jnp.sum(result.astype(jnp.float32).reshape(length // 8, 8, PAIR), axis=0)
        bsum[dp, :, aligned(j, PAIR)] += part
        vg[s, :, aligned(tok * pairs + j, PAIR)] = g_buf[s, aligned(tok, local), aligned(j, PAIR)]

    bsum[dp] = jnp.zeros_like(bias)

    def sequence(s, carry):
        pltpu.make_async_copy(
            teacher.at[s, :, aligned(tok, tcols)], t_full.at[s, aligned(tok, local), :], lsem.at[1 + s]
        ).wait()
        for k in range(1, n_tok):
            t_copy(s, k).wait_recv()
        for k in range(1, n_tok):
            s_copy(s, k).wait_recv()

        def pair(j, inner):
            unit(s, j)
            for k in range(1, n_tok):
                g_copy(s, j, k).start()
            return inner

        lax.fori_loop(0, pairs, pair, 0)
        return carry

    lax.fori_loop(0, seqs, sequence, 0)

    for k in range(1, n_dp):
        r_copy(k).start()

    out_block = min(256, width)

    def finish(s, carry):
        def arrive(j, inner):
            for k in range(1, n_tok):
                g_copy(s, j, k).wait_recv()
            return inner

        lax.fori_loop(0, pairs, arrive, 0)

        def columns(b, inner):
            out[s, :, aligned(b, out_block)] = lax.dot_general(
                vg[s], w_full[aligned(b, out_block), :], (((1,), (1,)), ((), ())),
                preferred_element_type=jnp.float32,
            ).astype(jnp.bfloat16)
            return inner

        lax.fori_loop(0, width // out_block, columns, 0)
        return carry

    lax.fori_loop(0, seqs, finish, 0)

    for k in range(1, n_dp):
        r_copy(k).wait_recv()
    total = bsum[0]
    for d in range(1, n_dp):
        total = total + bsum[d]
    total = jnp.sum(total, axis=0, keepdims=True) * (1.0 / math.sqrt(seqs * n_dp * length))
    bias_out[...] = jnp.broadcast_to(total, bias_out.shape)

    for k in range(1, n_tok):
        w_copy(k).wait_send()
        b_copy(k).wait_send()
        for s in range(seqs):
            t_copy(s, k).wait_send()
            s_copy(s, k).wait_send()

    def sent(j, carry):
        for s in range(seqs):
            for k in range(1, n_tok):
                g_copy(s, j, k).wait_send()
        return carry

    lax.fori_loop(0, pairs, sent, 0)
    for k in range(1, half):
        d_copy(k).wait_send()
    for k in range(half):
        c_copy(k).wait_send()
    for k in range(1, n_dp):
        r_copy(k).wait_send()


def body(student_hidden, teacher_values, value_weight, value_bias):
    seqs, local, width = student_hidden.shape
    n_tok = lax.axis_size("tok")
    n_dp = lax.axis_size("dp")
    cols = value_weight.shape[1]
    length = n_tok * local
    tcols = teacher_values.shape[2] // n_tok
    pairs = cols // PAIR
    rows = student_hidden.reshape(seqs * local, width)
    bias = jnp.broadcast_to(value_bias.astype(jnp.float32), (8, cols))
    dma = pltpu.SemaphoreType.DMA
    half = n_dp // 2
    bf16, f32 = jnp.bfloat16, jnp.float32
    hidden_grad, bias_grad = pl.pallas_call(
        functools.partial(kernel, n_tok, n_dp, seqs, local),
        out_shape=(
            jax.ShapeDtypeStruct((seqs, local, width), bf16),
            jax.ShapeDtypeStruct((8, cols), f32),
        ),
        in_specs=[
            pl.BlockSpec(memory_space=pltpu.VMEM),
            pl.BlockSpec(memory_space=pl.ANY),
            pl.BlockSpec(memory_space=pl.ANY),
            pl.BlockSpec(memory_space=pltpu.VMEM),
        ],
        out_specs=(pl.BlockSpec(memory_space=pltpu.VMEM),) * 2,
        scratch_shapes=[
            pltpu.VMEM((width, n_tok * cols), bf16),
            pltpu.VMEM((seqs, length, tcols), bf16),
            pltpu.VMEM((n_tok, seqs, local, cols), bf16),
            pltpu.VMEM((seqs, length, cols), bf16),
            pltpu.VMEM((seqs, length, cols), bf16),
            pltpu.VMEM((seqs, local, n_tok * cols), bf16),
            pltpu.VMEM((n_tok, 8, cols), f32),
            pltpu.VMEM((n_dp, 8, cols), f32),
            pltpu.VMEM((HEADS_PER, TH, length), bf16),
            pltpu.VMEM((PAIR, length), bf16),
            pltpu.VMEM((HEADS_PER, length, PAIR), bf16),
            pltpu.VMEM((length, PAIR), f32),
            pltpu.VMEM((PAIR, length), f32),
            dma((n_tok,)), dma((n_tok,)),
            dma((half,)), dma((half,)),
            dma((half,)), dma((half,)),
            dma((n_tok,)), dma((n_tok,)),
            dma((seqs, n_tok)), dma((seqs, n_tok)),
            dma((seqs, n_tok)), dma((seqs, n_tok)),
            dma((seqs, pairs, n_tok)), dma((seqs, pairs, n_tok)),
            dma((n_dp,)), dma((n_dp,)),
            dma((1 + seqs,)),
        ],
        compiler_params=pltpu.CompilerParams(
            collective_id=0, has_side_effects=True, vmem_limit_bytes=56 * 2**20
        ),
    )(rows, teacher_values, value_weight, bias)
    return hidden_grad, bias_grad[0]


def solution(mesh):
    placed = (P("dp", "tok", None), P("dp", "tok", None), P(None, "tok"), P(None, "tok"))
    return jax.shard_map(
        body,
        mesh=mesh,
        in_specs=placed,
        out_specs=(P("dp", "tok", None), P("tok")),
        check_vma=False,
    )
```

```python
import functools
import math

import jax
import jax.numpy as jnp
from jax import lax
from jax.experimental import pallas as pl
from jax.experimental.pallas import tpu as pltpu
from jax.sharding import PartitionSpec as P

SH = 64
TH = 128
PAIR = 128
HEADS_PER = PAIR // SH
LOG2E = math.log2(math.e)


def aligned(index, step):
    return pl.ds(pl.multiple_of(index * step, step), step)


def kernel(
    n_tok, n_dp, seqs, local,
    hidden, teacher, weight, bias,
    out, bias_out,
    w_full, t_full, s_send, s_full, g_buf, vg, bias_all, bsum,
    t_tr, s_tr, s_mask, acc, acc_tr,
    wsend, wrecv, dsend, drecv, csend, crecv, bsend, brecv,
    tsend, trecv, ssend, srecv, gsend, grecv, rsend, rrecv, lsem,
):
    tok = lax.axis_index("tok")
    dp = lax.axis_index("dp")
    width = hidden.shape[1]
    cols = weight.shape[1]
    tcols = teacher.shape[2] // n_tok
    length = n_tok * local
    slice_rows = width // n_dp
    pairs = cols // PAIR
    half = n_dp // 2
    core = lax.rem(dp, 2)
    sibling = dp + 1 - 2 * core

    def tok_at(k):
        return lax.rem(tok + k, n_tok)

    def same_core(k):
        return lax.rem(dp + 2 * k, n_dp)

    def remote(src, dst, send, recv, **where):
        return pltpu.make_async_remote_copy(
            src_ref=src, dst_ref=dst, send_sem=send, recv_sem=recv,
            device_id=where, device_id_type=pl.DeviceIdType.MESH,
        )

    def w_block(owner, q):
        return w_full.at[aligned(owner, slice_rows), aligned(q, cols)]

    def w_copy(q, step):
        src = weight.at[aligned(dp, slice_rows), :] if q is tok else w_block(dp, q)
        return remote(
            src, w_block(dp, q), wsend.at[(step + 1) // 2, q], wrecv.at[q], tok=lax.rem(tok + step + n_tok, n_tok)
        )

    def d_copy(q, m):
        block = w_block(dp, q)
        return remote(block, block, dsend.at[q, m], drecv.at[q, m], dp=same_core(m))

    def c_copy(q, m):
        block = w_block(lax.rem(dp - 2 * m + n_dp, n_dp), q)
        return remote(block, block, csend.at[q, m], crecv.at[q, m], dp=sibling)

    def b_copy(k):
        return remote(bias_all.at[tok], bias_all.at[tok], bsend.at[k], brecv.at[k], tok=tok_at(k))

    def t_copy(s, k):
        return remote(
            teacher.at[s, :, aligned(tok_at(k), tcols)],
            t_full.at[s, aligned(tok, local), :],
            tsend.at[s, k], trecv.at[s, k], tok=tok_at(k),
        )

    def s_copy(s, k):
        return remote(
            s_send.at[k, s], s_full.at[s, aligned(tok, local), :],
            ssend.at[s, k], srecv.at[s, k], tok=tok_at(k),
        )

    def g_copy(s, j, k):
        return remote(
            g_buf.at[s, aligned(tok_at(k), local), aligned(j, PAIR)],
            vg.at[s, :, aligned(tok * pairs + j, PAIR)],
            gsend.at[s, j, k], grecv.at[s, j, k], tok=tok_at(k),
        )

    def r_copy(k):
        return remote(bsum.at[dp], bsum.at[dp], rsend.at[k], rrecv.at[k], dp=lax.rem(dp + k, n_dp))

    def own_w():
        return pltpu.make_async_copy(weight, w_full.at[:, aligned(tok, cols)], lsem.at[0])

    def own_t(s):
        return pltpu.make_async_copy(
            teacher.at[s, :, aligned(tok, tcols)], t_full.at[s, aligned(tok, local), :], lsem.at[1 + s]
        )

    barrier = pltpu.get_barrier_semaphore()
    for k in range(1, n_tok):
        pl.semaphore_signal(barrier, inc=1, device_id={"tok": tok_at(k)}, device_id_type=pl.DeviceIdType.MESH)
    for k in range(1, n_dp):
        pl.semaphore_signal(
            barrier, inc=1, device_id={"dp": lax.rem(dp + k, n_dp)}, device_id_type=pl.DeviceIdType.MESH
        )
    bias_all[tok] = bias[...]
    own_w().start()
    for s in range(seqs):
        own_t(s).start()
    pl.semaphore_wait(barrier, n_tok + n_dp - 2)

    has_left, has_right = tok > 0, tok < n_tok - 1

    def pass_left(q):
        @pl.when(has_left)
        def _():
            w_copy(q, -1).start()

    def pass_right(q):
        @pl.when(has_right)
        def _():
            w_copy(q, 1).start()

    pass_left(tok)
    pass_right(tok)
    for k in range(1, n_tok):
        b_copy(k).start()

    def spread(q):
        for m in range(1, half):
            d_copy(q, m).start()
        c_copy(q, 0).start()

    def arrived(dist):
        @pl.when(tok - dist >= 0)
        def _():
            q = tok - dist
            w_copy(q, 1).wait_recv()
            pass_right(q)
            spread(q)

        @pl.when(tok + dist < n_tok)
        def _():
            q = tok + dist
            w_copy(q, -1).wait_recv()
            pass_left(q)
            spread(q)

    def start_teacher(s):
        for k in range(1, n_tok):
            t_copy(s, k).start()

    def project(s, k):
        p = tok_at(k)
        values = jnp.dot(
            hidden[s * local : (s + 1) * local, :], w_full[:, aligned(p, cols)], preferred_element_type=jnp.float32
        )
        return (values + bias_all[p][0:1, :]).astype(jnp.bfloat16)

    arrived(1)
    start_teacher(0)
    for dist in range(2, n_tok):
        arrived(dist)
    own_w().wait()
    for s in range(seqs):
        s_full[s, aligned(tok, local), :] = project(s, 0)

    def block_at(k):
        return lax.rem(tok - k + n_tok, n_tok)

    def forward(k, carry):
        for m in range(1, half):
            d_copy(block_at(k), m).wait_recv()
            c_copy(block_at(k), m).start()
        return carry

    lax.fori_loop(1, n_tok, forward, 0)
    for k in range(1, n_tok):
        b_copy(k).wait_recv()

    def first(k, carry):
        for m in range(half):
            c_copy(block_at(k), m).wait_recv()
        s_send[n_tok - k, 0] = project(0, n_tok - k)
        s_copy(0, n_tok - k).start()
        return carry

    lax.fori_loop(1, n_tok, first, 0)
    for s in range(1, seqs):
        start_teacher(s)

        def later(k, carry):
            s_send[k, s] = project(s, k)
            return carry

        lax.fori_loop(1, n_tok, later, 0)

    block = min(256, length)
    lane_head = lax.broadcasted_iota(jnp.int32, (length, PAIR), 1) // SH
    t_scale = LOG2E / math.sqrt(TH)
    s_scale = LOG2E / math.sqrt(SH)

    def softmax_terms(scores, scale):
        top = jnp.max(scores, axis=1, keepdims=True)
        terms = jnp.exp2((scores - top) * scale)
        return terms, length / jnp.sum(terms, axis=1, keepdims=True)

    def unit(s, j):
        values = s_full[s, :, aligned(j, PAIR)]
        s_tr[...] = values.T
        for h in range(HEADS_PER):
            s_mask[h] = jnp.where(lane_head == h, values, jnp.zeros_like(values))
            t_tr[h] = t_full[s, :, aligned(j * HEADS_PER + h, TH)].T
        acc_tr[...] = jnp.zeros_like(acc_tr)

        def query(i, carry):
            rows = aligned(i, block)
            total = None
            for h in range(HEADS_PER):
                t_scores = jnp.dot(
                    t_full[s, rows, aligned(j * HEADS_PER + h, TH)], t_tr[h], preferred_element_type=jnp.float32
                )
                s_scores = jnp.dot(s_mask[h, rows, :], s_tr[...], preferred_element_type=jnp.float32)
                t_terms, t_norm = softmax_terms(t_scores, t_scale)
                s_terms, s_norm = softmax_terms(s_scores, s_scale)
                grad = (s_terms * s_norm - t_terms * t_norm).astype(jnp.bfloat16)
                part = jnp.dot(grad, s_mask[h], preferred_element_type=jnp.float32)
                total = part if total is None else total + part
                acc_tr[h * SH : (h + 1) * SH, :] += jnp.dot(
                    s_tr[h * SH : (h + 1) * SH, rows], grad, preferred_element_type=jnp.float32
                )
            acc[rows, :] = total
            return carry

        lax.fori_loop(0, length // block, query, 0)
        result = ((acc[...] + acc_tr[...].T) * (1.0 / math.sqrt(SH))).astype(jnp.bfloat16)
        g_buf[s, :, aligned(j, PAIR)] = result
        part = jnp.sum(result.astype(jnp.float32).reshape(length // 8, 8, PAIR), axis=0)
        bsum[dp, :, aligned(j, PAIR)] += part
        vg[s, :, aligned(tok * pairs + j, PAIR)] = g_buf[s, aligned(tok, local), aligned(j, PAIR)]

    bsum[dp] = jnp.zeros_like(bias)

    def sequence(s, carry):
        pltpu.make_async_copy(
            teacher.at[s, :, aligned(tok, tcols)], t_full.at[s, aligned(tok, local), :], lsem.at[1 + s]
        ).wait()
        for k in range(1, n_tok):
            t_copy(s, k).wait_recv()
        for k in range(1, n_tok):
            s_copy(s, k).wait_recv()

        @pl.when(s + 1 < seqs)
        def _():
            for k in range(1, n_tok):
                s_copy(s + 1, k).start()

        def pair(j, inner):
            unit(s, j)
            for k in range(1, n_tok):
                g_copy(s, j, k).start()
            return inner

        lax.fori_loop(0, pairs, pair, 0)
        return carry

    lax.fori_loop(0, seqs, sequence, 0)

    for k in range(1, n_dp):
        r_copy(k).start()

    out_block = min(256, width)

    def finish(s, carry):
        def arrive(j, inner):
            for k in range(1, n_tok):
                g_copy(s, j, k).wait_recv()
            return inner

        lax.fori_loop(0, pairs, arrive, 0)

        def columns(b, inner):
            out[s, :, aligned(b, out_block)] = lax.dot_general(
                vg[s], w_full[aligned(b, out_block), :], (((1,), (1,)), ((), ())),
                preferred_element_type=jnp.float32,
            ).astype(jnp.bfloat16)
            return inner

        lax.fori_loop(0, width // out_block, columns, 0)
        return carry

    lax.fori_loop(0, seqs, finish, 0)

    for k in range(1, n_dp):
        r_copy(k).wait_recv()
    total = bsum[0]
    for d in range(1, n_dp):
        total = total + bsum[d]
    total = jnp.sum(total, axis=0, keepdims=True) * (1.0 / math.sqrt(seqs * n_dp * length))
    bias_out[...] = jnp.broadcast_to(total, bias_out.shape)

    for k in range(1, n_tok):
        b_copy(k).wait_send()
        for s in range(seqs):
            t_copy(s, k).wait_send()
            s_copy(s, k).wait_send()

    for q in range(n_tok):
        @pl.when((tok <= q) & has_left)
        def _():
            w_copy(q, -1).wait_send()

        @pl.when((tok >= q) & has_right)
        def _():
            w_copy(q, 1).wait_send()

    def sent(j, carry):
        for s in range(seqs):
            for k in range(1, n_tok):
                g_copy(s, j, k).wait_send()
        return carry

    lax.fori_loop(0, pairs, sent, 0)
    def passed(k, carry):
        for m in range(1, half):
            d_copy(block_at(k), m).wait_send()
        for m in range(half):
            c_copy(block_at(k), m).wait_send()
        return carry

    lax.fori_loop(1, n_tok, passed, 0)
    for k in range(1, n_dp):
        r_copy(k).wait_send()


def body(student_hidden, teacher_values, value_weight, value_bias):
    seqs, local, width = student_hidden.shape
    n_tok = lax.axis_size("tok")
    n_dp = lax.axis_size("dp")
    cols = value_weight.shape[1]
    length = n_tok * local
    tcols = teacher_values.shape[2] // n_tok
    pairs = cols // PAIR
    rows = student_hidden.reshape(seqs * local, width)
    bias = jnp.broadcast_to(value_bias.astype(jnp.float32), (8, cols))
    dma = pltpu.SemaphoreType.DMA
    half = n_dp // 2
    bf16, f32 = jnp.bfloat16, jnp.float32
    hidden_grad, bias_grad = pl.pallas_call(
        functools.partial(kernel, n_tok, n_dp, seqs, local),
        out_shape=(
            jax.ShapeDtypeStruct((seqs, local, width), bf16),
            jax.ShapeDtypeStruct((8, cols), f32),
        ),
        in_specs=[
            pl.BlockSpec(memory_space=pltpu.VMEM),
            pl.BlockSpec(memory_space=pl.ANY),
            pl.BlockSpec(memory_space=pl.ANY),
            pl.BlockSpec(memory_space=pltpu.VMEM),
        ],
        out_specs=(pl.BlockSpec(memory_space=pltpu.VMEM),) * 2,
        scratch_shapes=[
            pltpu.VMEM((width, n_tok * cols), bf16),
            pltpu.VMEM((seqs, length, tcols), bf16),
            pltpu.VMEM((n_tok, seqs, local, cols), bf16),
            pltpu.VMEM((seqs, length, cols), bf16),
            pltpu.VMEM((seqs, length, cols), bf16),
            pltpu.VMEM((seqs, local, n_tok * cols), bf16),
            pltpu.VMEM((n_tok, 8, cols), f32),
            pltpu.VMEM((n_dp, 8, cols), f32),
            pltpu.VMEM((HEADS_PER, TH, length), bf16),
            pltpu.VMEM((PAIR, length), bf16),
            pltpu.VMEM((HEADS_PER, length, PAIR), bf16),
            pltpu.VMEM((length, PAIR), f32),
            pltpu.VMEM((PAIR, length), f32),
            dma((2, n_tok)), dma((n_tok,)),
            dma((n_tok, half)), dma((n_tok, half)),
            dma((n_tok, half)), dma((n_tok, half)),
            dma((n_tok,)), dma((n_tok,)),
            dma((seqs, n_tok)), dma((seqs, n_tok)),
            dma((seqs, n_tok)), dma((seqs, n_tok)),
            dma((seqs, pairs, n_tok)), dma((seqs, pairs, n_tok)),
            dma((n_dp,)), dma((n_dp,)),
            dma((1 + seqs,)),
        ],
        compiler_params=pltpu.CompilerParams(
            collective_id=0, has_side_effects=True, vmem_limit_bytes=56 * 2**20
        ),
    )(rows, teacher_values, value_weight, bias)
    return hidden_grad, bias_grad[0]


def solution(mesh):
    placed = (P("dp", "tok", None), P("dp", "tok", None), P(None, "tok"), P(None, "tok"))
    return jax.shard_map(
        body,
        mesh=mesh,
        in_specs=placed,
        out_specs=(P("dp", "tok", None), P("tok")),
        check_vma=False,
    )
```

```python
import functools
import math

import jax
import jax.numpy as jnp
from jax import lax
from jax.experimental import pallas as pl
from jax.experimental.pallas import tpu as pltpu
from jax.sharding import PartitionSpec as P

SH = 64
TH = 128
PAIR = 128
HEADS_PER = PAIR // SH
LOG2E = math.log2(math.e)


def aligned(index, step):
    return pl.ds(pl.multiple_of(index * step, step), step)


def kernel(
    n_tok, n_dp, seqs, local,
    hidden, teacher, weight, bias,
    out, bias_out,
    w_full, t_full, s_send, s_full, g_buf, vg, bias_all, bsum,
    t_tr, s_tr, s_mask, acc, acc_tr,
    wsend, wrecv, dsend, drecv, csend, crecv, bsend, brecv,
    tsend, trecv, ssend, srecv, gsend, grecv, rsend, rrecv, lsem,
):
    tok = lax.axis_index("tok")
    dp = lax.axis_index("dp")
    width = hidden.shape[1]
    cols = weight.shape[1]
    tcols = teacher.shape[2] // n_tok
    length = n_tok * local
    slice_rows = width // n_dp
    pairs = cols // PAIR
    half = n_dp // 2
    core = lax.rem(dp, 2)
    sibling = dp + 1 - 2 * core

    def tok_at(k):
        return lax.rem(tok + k, n_tok)

    def same_core(k):
        return lax.rem(dp + 2 * k, n_dp)

    def remote(src, dst, send, recv, **where):
        return pltpu.make_async_remote_copy(
            src_ref=src, dst_ref=dst, send_sem=send, recv_sem=recv,
            device_id=where, device_id_type=pl.DeviceIdType.MESH,
        )

    def w_block(owner, q):
        return w_full.at[aligned(owner, slice_rows), aligned(q, cols)]

    def w_copy(q, step):
        src = weight.at[aligned(dp, slice_rows), :] if q is tok else w_block(dp, q)
        return remote(
            src, w_block(dp, q), wsend.at[(step + 1) // 2, q], wrecv.at[q], tok=lax.rem(tok + step + n_tok, n_tok)
        )

    def d_copy(q, m):
        block = w_block(dp, q)
        return remote(block, block, dsend.at[q, m], drecv.at[q, m], dp=same_core(m))

    def c_copy(q, m):
        block = w_block(lax.rem(dp - 2 * m + n_dp, n_dp), q)
        return remote(block, block, csend.at[q, m], crecv.at[q, m], dp=sibling)

    def b_copy(k):
        return remote(bias_all.at[tok], bias_all.at[tok], bsend.at[k], brecv.at[k], tok=tok_at(k))

    def t_copy(s, k):
        return remote(
            teacher.at[s, :, aligned(tok_at(k), tcols)],
            t_full.at[s, aligned(tok, local), :],
            tsend.at[s, k], trecv.at[s, k], tok=tok_at(k),
        )

    def s_copy(s, k):
        return remote(
            s_send.at[k, s], s_full.at[s, aligned(tok, local), :],
            ssend.at[s, k], srecv.at[s, k], tok=tok_at(k),
        )

    def g_copy(s, j, k):
        return remote(
            g_buf.at[s, aligned(tok_at(k), local), aligned(j, PAIR)],
            vg.at[s, :, aligned(tok * pairs + j, PAIR)],
            gsend.at[s, j, k], grecv.at[s, j, k], tok=tok_at(k),
        )

    def r_copy(k):
        return remote(bsum.at[dp], bsum.at[dp], rsend.at[k], rrecv.at[k], dp=lax.rem(dp + k, n_dp))

    def own_w():
        return pltpu.make_async_copy(weight, w_full.at[:, aligned(tok, cols)], lsem.at[0])

    def own_t(s):
        return pltpu.make_async_copy(
            teacher.at[s, :, aligned(tok, tcols)], t_full.at[s, aligned(tok, local), :], lsem.at[1 + s]
        )

    barrier = pltpu.get_barrier_semaphore()
    for k in range(1, n_tok):
        pl.semaphore_signal(barrier, inc=1, device_id={"tok": tok_at(k)}, device_id_type=pl.DeviceIdType.MESH)
    for k in range(1, n_dp):
        pl.semaphore_signal(
            barrier, inc=1, device_id={"dp": lax.rem(dp + k, n_dp)}, device_id_type=pl.DeviceIdType.MESH
        )
    bias_all[tok] = bias[...]
    own_w().start()
    for s in range(seqs):
        own_t(s).start()
    pl.semaphore_wait(barrier, n_tok + n_dp - 2)

    has_left, has_right = tok > 0, tok < n_tok - 1

    def pass_left(q):
        @pl.when(has_left)
        def _():
            w_copy(q, -1).start()

    def pass_right(q):
        @pl.when(has_right)
        def _():
            w_copy(q, 1).start()

    pass_left(tok)
    pass_right(tok)
    for k in range(1, n_tok):
        b_copy(k).start()

    def spread(q):
        for m in range(1, half):
            d_copy(q, m).start()
        c_copy(q, 0).start()

    def arrived(dist):
        @pl.when(tok - dist >= 0)
        def _():
            q = tok - dist
            w_copy(q, 1).wait_recv()
            pass_right(q)
            spread(q)

        @pl.when(tok + dist < n_tok)
        def _():
            q = tok + dist
            w_copy(q, -1).wait_recv()
            pass_left(q)
            spread(q)

    def start_teacher(s):
        for k in range(1, n_tok):
            t_copy(s, k).start()

    def project(s, k):
        p = tok_at(k)
        values = jnp.dot(
            hidden[s * local : (s + 1) * local, :], w_full[:, aligned(p, cols)], preferred_element_type=jnp.float32
        )
        return (values + bias_all[p][0:1, :]).astype(jnp.bfloat16)

    arrived(1)
    start_teacher(0)
    for dist in range(2, n_tok):
        arrived(dist)
    for s in range(1, seqs):
        start_teacher(s)
    own_w().wait()
    for s in range(seqs):
        s_full[s, aligned(tok, local), :] = project(s, 0)

    def block_at(k):
        return lax.rem(tok - k + n_tok, n_tok)

    def forward(k, carry):
        for m in range(1, half):
            d_copy(block_at(k), m).wait_recv()
            c_copy(block_at(k), m).start()
        return carry

    lax.fori_loop(1, n_tok, forward, 0)
    for k in range(1, n_tok):
        b_copy(k).wait_recv()

    def first(k, carry):
        for m in range(half):
            c_copy(block_at(k), m).wait_recv()
        s_send[n_tok - k, 0] = project(0, n_tok - k)
        s_copy(0, n_tok - k).start()
        return carry

    lax.fori_loop(1, n_tok, first, 0)
    for s in range(1, seqs):
        def later(k, carry):
            s_send[k, s] = project(s, k)
            return carry

        lax.fori_loop(1, n_tok, later, 0)

    block = min(256, length)
    lane_head = lax.broadcasted_iota(jnp.int32, (length, PAIR), 1) // SH
    t_scale = LOG2E / math.sqrt(TH)
    s_scale = LOG2E / math.sqrt(SH)

    def softmax_terms(scores, scale):
        top = jnp.max(scores, axis=1, keepdims=True)
        terms = jnp.exp2((scores - top) * scale)
        return terms, length / jnp.sum(terms, axis=1, keepdims=True)

    def unit(s, j):
        values = s_full[s, :, aligned(j, PAIR)]
        s_tr[...] = values.T
        for h in range(HEADS_PER):
            s_mask[h] = jnp.where(lane_head == h, values, jnp.zeros_like(values))
            t_tr[h] = t_full[s, :, aligned(j * HEADS_PER + h, TH)].T
        acc_tr[...] = jnp.zeros_like(acc_tr)

        def query(i, carry):
            rows = aligned(i, block)
            total = None
            for h in range(HEADS_PER):
                t_scores = jnp.dot(
                    t_full[s, rows, aligned(j * HEADS_PER + h, TH)], t_tr[h], preferred_element_type=jnp.float32
                )
                s_scores = jnp.dot(s_mask[h, rows, :], s_tr[...], preferred_element_type=jnp.float32)
                t_terms, t_norm = softmax_terms(t_scores, t_scale)
                s_terms, s_norm = softmax_terms(s_scores, s_scale)
                grad = (s_terms * s_norm - t_terms * t_norm).astype(jnp.bfloat16)
                part = jnp.dot(grad, s_mask[h], preferred_element_type=jnp.float32)
                total = part if total is None else total + part
                acc_tr[h * SH : (h + 1) * SH, :] += jnp.dot(
                    s_tr[h * SH : (h + 1) * SH, rows], grad, preferred_element_type=jnp.float32
                )
            acc[rows, :] = total
            return carry

        lax.fori_loop(0, length // block, query, 0)
        result = ((acc[...] + acc_tr[...].T) * (1.0 / math.sqrt(SH))).astype(jnp.bfloat16)
        g_buf[s, :, aligned(j, PAIR)] = result
        part = jnp.sum(result.astype(jnp.float32).reshape(length // 8, 8, PAIR), axis=0)
        bsum[dp, :, aligned(j, PAIR)] += part
        vg[s, :, aligned(tok * pairs + j, PAIR)] = g_buf[s, aligned(tok, local), aligned(j, PAIR)]

    bsum[dp] = jnp.zeros_like(bias)

    def sequence(s, carry):
        pltpu.make_async_copy(
            teacher.at[s, :, aligned(tok, tcols)], t_full.at[s, aligned(tok, local), :], lsem.at[1 + s]
        ).wait()
        for k in range(1, n_tok):
            t_copy(s, k).wait_recv()
        for k in range(1, n_tok):
            s_copy(s, k).wait_recv()

        @pl.when(s + 1 < seqs)
        def _():
            for k in range(1, n_tok):
                s_copy(s + 1, k).start()

        def pair(j, inner):
            unit(s, j)
            for k in range(1, n_tok):
                g_copy(s, j, k).start()
            return inner

        lax.fori_loop(0, pairs, pair, 0)
        return carry

    lax.fori_loop(0, seqs, sequence, 0)

    for k in range(1, n_dp):
        r_copy(k).start()

    out_block = min(256, width)

    def finish(s, carry):
        def arrive(j, inner):
            for k in range(1, n_tok):
                g_copy(s, j, k).wait_recv()
            return inner

        lax.fori_loop(0, pairs, arrive, 0)

        def columns(b, inner):
            out[s, :, aligned(b, out_block)] = lax.dot_general(
                vg[s], w_full[aligned(b, out_block), :], (((1,), (1,)), ((), ())),
                preferred_element_type=jnp.float32,
            ).astype(jnp.bfloat16)
            return inner

        lax.fori_loop(0, width // out_block, columns, 0)
        return carry

    lax.fori_loop(0, seqs, finish, 0)

    for k in range(1, n_dp):
        r_copy(k).wait_recv()
    total = bsum[0]
    for d in range(1, n_dp):
        total = total + bsum[d]
    total = jnp.sum(total, axis=0, keepdims=True) * (1.0 / math.sqrt(seqs * n_dp * length))
    bias_out[...] = jnp.broadcast_to(total, bias_out.shape)

    for k in range(1, n_tok):
        b_copy(k).wait_send()
        for s in range(seqs):
            t_copy(s, k).wait_send()
            s_copy(s, k).wait_send()

    for q in range(n_tok):
        @pl.when((tok <= q) & has_left)
        def _():
            w_copy(q, -1).wait_send()

        @pl.when((tok >= q) & has_right)
        def _():
            w_copy(q, 1).wait_send()

    def sent(j, carry):
        for s in range(seqs):
            for k in range(1, n_tok):
                g_copy(s, j, k).wait_send()
        return carry

    lax.fori_loop(0, pairs, sent, 0)
    def passed(k, carry):
        for m in range(1, half):
            d_copy(block_at(k), m).wait_send()
        for m in range(half):
            c_copy(block_at(k), m).wait_send()
        return carry

    lax.fori_loop(1, n_tok, passed, 0)
    for k in range(1, n_dp):
        r_copy(k).wait_send()


def body(student_hidden, teacher_values, value_weight, value_bias):
    seqs, local, width = student_hidden.shape
    n_tok = lax.axis_size("tok")
    n_dp = lax.axis_size("dp")
    cols = value_weight.shape[1]
    length = n_tok * local
    tcols = teacher_values.shape[2] // n_tok
    pairs = cols // PAIR
    rows = student_hidden.reshape(seqs * local, width)
    bias = jnp.broadcast_to(value_bias.astype(jnp.float32), (8, cols))
    dma = pltpu.SemaphoreType.DMA
    half = n_dp // 2
    bf16, f32 = jnp.bfloat16, jnp.float32
    hidden_grad, bias_grad = pl.pallas_call(
        functools.partial(kernel, n_tok, n_dp, seqs, local),
        out_shape=(
            jax.ShapeDtypeStruct((seqs, local, width), bf16),
            jax.ShapeDtypeStruct((8, cols), f32),
        ),
        in_specs=[
            pl.BlockSpec(memory_space=pltpu.VMEM),
            pl.BlockSpec(memory_space=pl.ANY),
            pl.BlockSpec(memory_space=pl.ANY),
            pl.BlockSpec(memory_space=pltpu.VMEM),
        ],
        out_specs=(pl.BlockSpec(memory_space=pltpu.VMEM),) * 2,
        scratch_shapes=[
            pltpu.VMEM((width, n_tok * cols), bf16),
            pltpu.VMEM((seqs, length, tcols), bf16),
            pltpu.VMEM((n_tok, seqs, local, cols), bf16),
            pltpu.VMEM((seqs, length, cols), bf16),
            pltpu.VMEM((seqs, length, cols), bf16),
            pltpu.VMEM((seqs, local, n_tok * cols), bf16),
            pltpu.VMEM((n_tok, 8, cols), f32),
            pltpu.VMEM((n_dp, 8, cols), f32),
            pltpu.VMEM((HEADS_PER, TH, length), bf16),
            pltpu.VMEM((PAIR, length), bf16),
            pltpu.VMEM((HEADS_PER, length, PAIR), bf16),
            pltpu.VMEM((length, PAIR), f32),
            pltpu.VMEM((PAIR, length), f32),
            dma((2, n_tok)), dma((n_tok,)),
            dma((n_tok, half)), dma((n_tok, half)),
            dma((n_tok, half)), dma((n_tok, half)),
            dma((n_tok,)), dma((n_tok,)),
            dma((seqs, n_tok)), dma((seqs, n_tok)),
            dma((seqs, n_tok)), dma((seqs, n_tok)),
            dma((seqs, pairs, n_tok)), dma((seqs, pairs, n_tok)),
            dma((n_dp,)), dma((n_dp,)),
            dma((1 + seqs,)),
        ],
        compiler_params=pltpu.CompilerParams(
            collective_id=0, has_side_effects=True, vmem_limit_bytes=56 * 2**20
        ),
    )(rows, teacher_values, value_weight, bias)
    return hidden_grad, bias_grad[0]


def solution(mesh):
    placed = (P("dp", "tok", None), P("dp", "tok", None), P(None, "tok"), P(None, "tok"))
    return jax.shard_map(
        body,
        mesh=mesh,
        in_specs=placed,
        out_specs=(P("dp", "tok", None), P("tok")),
        check_vma=False,
    )
```
